512 devices in a mesh: pipe: 16 (over y, x_hi, core), expert: 32 (over z, x_lo).
Axes of the slice: x: 4 (x_hi: 2, x_lo: 2; x = x_hi * 2 + x_lo), y: 4, z: 16, core: 2. Of those that a mesh axis runs over, the one named last changes fastest.
Arguments:
- tokens: bfloat16 [16, 4096, 3584], P('pipe', 'expert'), may hold values from -6 to 6
- expert_ids: int32 [16, 4096, 8], P('pipe', 'expert'), may hold values from 0 to 255, as said below
- gates: float32 [16, 4096, 8], P('pipe', 'expert'), may hold values from 0.1 to 1
- loss_weight: float32 [16, 4096], P('pipe', 'expert'), may hold values from 0.25 to 4
- w_gate: bfloat16 [16, 3584, 4096], P('pipe', None, 'expert'), may hold values from -0.09375 to 0.09375
- w_up: bfloat16 [16, 3584, 4096], P('pipe', None, 'expert'), may hold values from -0.09375 to 0.09375
- w_down: bfloat16 [16, 4096, 3584], P('pipe', 'expert'), may hold values from -0.1875 to 0.1875
Outputs:
- mixed: bfloat16 [16, 4096, 3584], P('pipe', 'expert')
- down_grad: bfloat16 [16, 4096, 1792], P('pipe', 'expert')
The draws below stay inside these ranges and needn't reach their ends.
Inputs may be any that keep to these rules, and one draw needn't show every extreme that they name: `expert_ids`: each token names 8 different experts. In every block of 128 tokens of one section slot, each expert below 4 is named by 1 to 16 tokens; for each section slot one of these experts is named by exactly 16 tokens in every block.
All inputs are finite; a program needn't handle non-finite values.
Results may differ from the reference program's by a relative error of at most 0.0074.
Values may be sent and summed in bfloat16 or wider, within the bound.
No kernel may reach another device: no remote copies, remote signals or barrier semaphores. Data moves between devices by JAX's collectives and lax.ppermute only.
A program may use at most 64 MiB of HBM per device.

```python
import math
import jax
import jax.numpy as jnp
from jax import lax

D = 3584
HID_DEV = 128
SPLIT = 8
ALL_EXPERTS = 256
TOPK = 8
TOK_DEV = 128
CAP = 16
EXPERT_HID = 1024
TOKENS = 4096
FF_ALL = 4096
N_PIPE = 16
N_EXPERT = 32


def slot_ids(key):
    blocks = TOKENS // TOK_DEV
    window = N_EXPERT // SPLIT
    subkeys = jax.random.split(key, 4)
    hottest = jax.random.randint(subkeys[0], (), 0, window)
    counts = jax.random.randint(subkeys[1], (blocks, window), 1, CAP + 1)
    counts = jnp.where(jnp.arange(window)[None, :] == hottest, CAP, counts)
    scores = jax.random.randint(subkeys[2], (blocks, window, TOK_DEV), 0, 1 << 20) * TOK_DEV + jnp.arange(TOK_DEV)
    ranking = jnp.argsort(jnp.argsort(scores, axis=-1), axis=-1)
    member = ranking < counts[:, :, None]
    member = jnp.transpose(member, (0, 2, 1)).reshape(TOKENS, window)
    window_count = jnp.sum(member.astype(jnp.int32), axis=-1)
    outside_count = ALL_EXPERTS - window
    outside_score = jax.random.randint(subkeys[3], (TOKENS, outside_count), 0, 1 << 20) * outside_count + jnp.arange(outside_count)
    outside_ids = jnp.argsort(outside_score, axis=-1)[:, :TOPK] + window
    window_rank = jnp.cumsum(member.astype(jnp.int32), axis=-1) - 1
    columns = []
    for column in range(TOPK):
        inside = jnp.sum(jnp.where(member & (window_rank == column), jnp.arange(window)[None, :], 0), axis=-1)
        chosen = jnp.clip(column - window_count, 0, TOPK - 1)
        outside = jnp.take_along_axis(outside_ids, chosen[:, None], axis=1)[:, 0]
        columns.append(jnp.where(column < window_count, inside, outside))
    return jnp.stack(columns, axis=-1).astype(jnp.int32)


def draw_expert_ids(key, part):
    key = jax.random.fold_in(key, 11)
    section_keys = jax.random.split(key, N_PIPE)
    return jax.vmap(slot_ids)(section_keys)


def shard_levels(key, extent, cuts, least, largest):
    loudness = 1.0
    for axis_at, shards_of in cuts:
        draws = jax.random.uniform(jax.random.fold_in(jax.random.fold_in(key, 6), axis_at), (shards_of,), jnp.float32, least / len(cuts), largest / len(cuts))
        loudness = loudness * jnp.repeat(jnp.exp(draws), extent[axis_at] // shards_of).reshape((-1,) + (1,) * (len(extent) - 1 - axis_at))
    return loudness


def centred(own_key, extent, scale, limit, shards=(), kind=jnp.bfloat16):
    entries = scale * jax.random.normal(own_key, extent, jnp.float32)
    if shards:
        entries = entries * shard_levels(own_key, extent, shards, -0.22, 0.18)
    return jnp.clip(entries, -limit, limit).astype(kind)


def setup_inputs(seed: int = 0) -> dict:
    keys = jax.random.split(jax.random.key(seed), 8)
    tokens = centred(keys[0], (N_PIPE, TOKENS, D), 1.0, 6.0, ((0, 16), (1, 32)))
    expert_ids = draw_expert_ids(jax.random.fold_in(keys[7], 71), 0)
    gates = jnp.clip(0.1 + 0.9 * jax.random.uniform(keys[2], (N_PIPE, TOKENS, TOPK), jnp.float32) ** shard_levels(keys[2], (N_PIPE, TOKENS, TOPK), ((0, 16), (1, 32)), -0.2, 0.2), 0.1, 1.0)
    loss_weight = jnp.clip(jnp.exp(math.log(4.0) - 2.7725887 * jax.random.uniform(keys[3], (N_PIPE, TOKENS), jnp.float32) ** shard_levels(keys[3], (N_PIPE, TOKENS), ((0, 16), (1, 32)), -0.2, 0.2)), 0.25, 4.0)
    w_gate = centred(keys[4], (N_PIPE, D, FF_ALL), D ** -0.5, 0.09375, ((0, 16), (2, 32)))
    w_up = centred(keys[5], (N_PIPE, D, FF_ALL), D ** -0.5, 0.09375, ((0, 16), (2, 32)))
    w_down = centred(keys[6], (N_PIPE, FF_ALL, D), EXPERT_HID ** -0.5, 0.1875, ((0, 16), (1, 32)))
    return dict(tokens=tokens, expert_ids=expert_ids, gates=gates, loss_weight=loss_weight, w_gate=w_gate, w_up=w_up, w_down=w_down)


def section_slot(tokens, routed, gate_vals, weighting, gate_cols, up_cols, down_rows):
    window = N_EXPERT // SPLIT
    blocks = N_EXPERT
    routed_b = routed.reshape(blocks, TOK_DEV, TOPK)
    gate_b = gate_vals.reshape(blocks, TOK_DEV, TOPK)
    experts = jnp.arange(window, dtype=jnp.int32)
    hits = routed_b[..., None] == experts
    member = jnp.any(hits, axis=2)
    weights = jnp.sum(jnp.where(hits, gate_b[..., None], jnp.float32(0.0)), axis=2)
    ranking = jnp.cumsum(member.astype(jnp.int32), axis=1) - 1
    matched = member[..., None] & (ranking[..., None] == jnp.arange(CAP, dtype=jnp.int32))
    positions = jnp.arange(TOK_DEV, dtype=jnp.int32)[None, :, None, None]
    offsets = (jnp.arange(blocks, dtype=jnp.int32) * TOK_DEV)[:, None, None]
    token_index = (jnp.sum(jnp.where(matched, positions, 0), axis=1) + offsets).astype(jnp.int32)
    slot_gate = jnp.sum(jnp.where(matched, weights[..., None], jnp.float32(0.0)), axis=1)
    filled = jnp.any(matched, axis=1)
    selected = jnp.where(filled[..., None], tokens[token_index], jnp.zeros((), jnp.bfloat16))
    per_expert = jnp.transpose(selected, (1, 0, 2, 3)).reshape(window, blocks * CAP, D)
    width = SPLIT * HID_DEV

    def forward(inputs):
        expert, rows_in = inputs
        start = expert * width
        gate_part = lax.dynamic_slice_in_dim(gate_cols, start, width, 1)
        up_part = lax.dynamic_slice_in_dim(up_cols, start, width, 1)
        gate_act = jnp.dot(rows_in, gate_part, preferred_element_type=jnp.float32)
        up_act = jnp.dot(rows_in, up_part, preferred_element_type=jnp.float32)
        hidden = (jax.nn.silu(gate_act) * up_act).astype(jnp.bfloat16)
        down_part = lax.dynamic_slice_in_dim(down_rows, start, width, 0).reshape(SPLIT, HID_DEV, D)
        pieces = jnp.einsum("rsh,shd->srd", hidden.reshape(-1, SPLIT, HID_DEV).astype(jnp.float32),
                            down_part.astype(jnp.float32), precision=lax.Precision.HIGHEST)
        rounded = lax.optimization_barrier(pieces.astype(jnp.bfloat16))
        combined = jnp.sum(rounded.astype(jnp.float32), axis=0)
        return combined, hidden

    combined, hidden = lax.map(forward, (experts, per_expert))
    gate_slots = jnp.transpose(slot_gate, (1, 0, 2)).reshape(window, blocks * CAP)
    index_slots = jnp.transpose(token_index, (1, 0, 2)).reshape(window, blocks * CAP)
    contrib = (gate_slots[..., None] * combined).reshape(-1, D)
    mixed = jnp.zeros((TOKENS, D), jnp.float32).at[index_slots.reshape(-1)].add(contrib)
    output = mixed.astype(jnp.bfloat16)
    slope = weighting[:, None] * output.astype(jnp.float32)
    cotan = (gate_slots[..., None] * slope[index_slots]).astype(jnp.bfloat16)
    grads = jnp.einsum("erh,erd->ehd", hidden.astype(jnp.float32), cotan.astype(jnp.float32),
                       precision=lax.Precision.HIGHEST)
    return output, grads.reshape(window * width, D)


def reference(tokens, expert_ids, gates, loss_weight, w_gate, w_up, w_down):
    def one_slot(inputs):
        return section_slot(*inputs)

    outputs, grads = lax.map(one_slot, (tokens, expert_ids, gates, loss_weight, w_gate, w_up, w_down))
    paired = grads + jnp.roll(grads, N_PIPE // 2, axis=0)
    half_pipe = N_PIPE // 2
    half_width = D // 2
    shares = jnp.concatenate([paired[:half_pipe, :, :half_width], paired[half_pipe:, :, half_width:]], axis=0)
    return outputs, shares.astype(jnp.bfloat16)
```

```python
import jax
import jax.numpy as jnp
from jax import lax
from jax.sharding import PartitionSpec as P

SPLIT = 8
CAP = 16
QUADS = 4
BF16 = jnp.bfloat16
F32 = jnp.float32


def segment_shift(block, distance):
    count = lax.axis_size("expert")
    step = (distance * SPLIT) % count
    if step == 0:
        return block
    return lax.ppermute(block, "expert", [(i, (i + step) % count) for i in range(count)])


def quad_from(block, distance):
    if distance % QUADS == 0:
        return block
    count = lax.axis_size("expert")
    route = []
    for i in range(count):
        base, place, side = i // SPLIT * SPLIT, i % SPLIT // 2, i % 2
        source = base + (place + distance) % QUADS * 2 + side
        route.append((source, i))
    return lax.ppermute(block, "expert", route)


def cross_pair(block, flip_side, flip_pipe):
    pipes, count = lax.axis_size("pipe"), lax.axis_size("expert")
    route = []
    for p in range(pipes):
        for i in range(count):
            other = (p + pipes // 2) % pipes if flip_pipe else p
            route.append((p * count + i, other * count + (i ^ 1 if flip_side else i)))
    return lax.ppermute(block, ("pipe", "expert"), route)


def routing(routed, gate_vals, experts):
    hits = routed[:, :, None] == experts[None, None, :]
    weights = jnp.sum(jnp.where(hits, gate_vals[:, :, None], jnp.float32(0.0)), axis=1)
    member = jnp.any(hits, axis=1)
    ranking = jnp.cumsum(member.astype(jnp.int32), axis=0) - 1
    ranking = jnp.where(member, ranking, CAP)
    return weights, ranking


def matching(ranking):
    slots = jnp.arange(CAP, dtype=jnp.int32)
    return ranking[..., None] == slots


def pick(array, index):
    return lax.dynamic_index_in_dim(array, index, 0, keepdims=False)


def per_device(tokens, expert_ids, gates, loss_weight, w_gate, w_up, w_down):
    tok_rows = tokens[0]
    tok_count, width = tok_rows.shape
    units = w_down.shape[1]
    experts = lax.axis_size("expert") // SPLIT
    eighth = width // 8
    place = lax.axis_index("expert")
    segment = place // SPLIT
    quad = place % SPLIT // 2
    half = lax.axis_index("pipe") // (lax.axis_size("pipe") // 2)

    gate_up = jnp.concatenate([w_gate[0], w_up[0]], axis=1)
    gate_up_other = cross_pair(gate_up, True, False)

    near = (segment + jnp.arange(experts, dtype=jnp.int32)) % experts
    weights, ranking = routing(expert_ids[0], gates[0], near)
    selector = matching(ranking).reshape(tok_count, experts * CAP)
    picked = jnp.dot(selector.astype(BF16).T, tok_rows, preferred_element_type=F32).astype(BF16)
    picked = picked.reshape(experts, CAP, width)
    rows = jnp.stack([segment_shift(picked[j], j) for j in range(experts)])
    rows = jnp.stack([quad_from(rows, r) for r in range(QUADS)]).reshape(-1, width)

    meta = jnp.concatenate(
        [weights.T, ranking.astype(F32).T, loss_weight, jnp.zeros((16 - 2 * experts - 1, tok_count), F32)]
    )
    metas = jnp.stack([quad_from(meta, r) for r in range(QUADS)])

    def act(both):
        acts = jnp.dot(rows, both, preferred_element_type=F32)
        return (jax.nn.silu(acts[:, :units]) * acts[:, units:]).astype(BF16)

    hidden = jnp.concatenate([act(gate_up), act(gate_up_other)], axis=1)
    hidden = hidden.reshape(QUADS, -1, 2 * units)
    hidden = jnp.concatenate(
        [jnp.roll(quad_from(hidden, r), r, axis=0) for r in range(QUADS)], axis=2
    ).reshape(-1, QUADS * 2 * units)

    quarters = w_down[0].T.reshape(2, QUADS, eighth, units).transpose(1, 0, 2, 3)
    quarters = quarters.reshape(QUADS, 2 * eighth, units)
    down_own = jnp.stack([quad_from(pick(quarters, (quad - r) % QUADS), r) for r in range(QUADS)])
    down_other = cross_pair(down_own, True, False)
    down = jnp.stack([down_own, down_other], axis=1)
    down = down.transpose(2, 0, 1, 3).reshape(2 * eighth, QUADS * 2 * units)
    out = lax.dot_general(
        hidden, down, (((1,), (1,)), ((), ())), preferred_element_type=F32
    ).astype(BF16)
    out = out.reshape(QUADS, experts, CAP, 2 * eighth)
    back = jnp.stack([segment_shift(out[:, j], -j) for j in range(experts)], axis=1)
    back = back.reshape(QUADS, experts * CAP, 2 * eighth)

    weight_r = metas[:, :experts]
    rank_r = metas[:, experts : 2 * experts].astype(jnp.int32)
    loss_r = metas[:, 2 * experts]
    spread = jnp.where(matching(rank_r), weight_r[..., None], jnp.float32(0.0))
    spread = spread.transpose(0, 2, 1, 3).reshape(QUADS, tok_count, experts * CAP)
    mixed = jnp.einsum(
        "rts,rsd->rtd", spread, back.astype(F32), precision=lax.Precision.HIGHEST,
        preferred_element_type=F32,
    ).astype(BF16)
    slope = loss_r[:, :, None] * mixed.astype(F32)
    cotan = jnp.einsum(
        "rts,rtd->rsd", spread, slope, precision=lax.Precision.HIGHEST, preferred_element_type=F32
    ).astype(BF16)
    cotan = cotan.reshape(QUADS, experts, CAP, 2 * eighth)
    cotan = jnp.stack([segment_shift(cotan[:, j], j) for j in range(experts)], axis=1)
    cotan = cotan.reshape(-1, 2 * eighth)

    pieces = jnp.stack([quad_from(mixed[-r % QUADS], r) for r in range(QUADS)])
    pieces = jnp.roll(pieces, quad, axis=0).reshape(QUADS, tok_count, 2, eighth)
    output = pieces.transpose(1, 2, 0, 3).reshape(tok_count, width)

    grads = lax.dot_general(cotan, hidden, (((0,), (0,)), ((), ())), preferred_element_type=F32)
    grads = grads.reshape(2, eighth, QUADS, 2, units).transpose(0, 3, 1, 2, 4)
    keep, give = pick(grads, half), pick(grads, 1 - half)
    total = (
        keep[0]
        + cross_pair(keep[1].astype(BF16), True, False).astype(F32)
        + cross_pair(give[0].astype(BF16), False, True).astype(F32)
        + cross_pair(give[1].astype(BF16), True, True).astype(F32)
    )
    share = total.astype(BF16)
    share = jnp.stack([quad_from(share[:, -r % QUADS], r) for r in range(QUADS)])
    share = jnp.roll(share, quad, axis=0).reshape(QUADS * eighth, units).T
    return output[None], share[None]


def solution(mesh):
    in_specs = (
        P("pipe", "expert", None),
        P("pipe", "expert", None),
        P("pipe", "expert", None),
        P("pipe", "expert"),
        P("pipe", None, "expert"),
        P("pipe", None, "expert"),
        P("pipe", "expert", None),
    )
    out_specs = (P("pipe", "expert", None), P("pipe", "expert", None))
    return jax.shard_map(
        per_device, mesh=mesh, in_specs=in_specs, out_specs=out_specs, check_vma=False
    )
```

```python
import functools

import jax
import jax.numpy as jnp
from jax import lax
from jax.experimental import pallas as pl
from jax.experimental.pallas import tpu as pltpu
from jax.sharding import PartitionSpec as P

SPLIT = 8
CAP = 16
QUADS = 4
BF16 = jnp.bfloat16
F32 = jnp.float32
VMEM_LIMIT = 48 * 1024 * 1024


def columns(count):
    return [[i for i in range(count) if i % 2 == side] for side in range(2)]


def quads(count):
    return [
        [base + 2 * place + side for place in range(QUADS)]
        for base in range(0, count, SPLIT)
        for side in range(2)
    ]


def exchange(blocks, axis, groups):
    return lax.all_to_all(blocks, axis, 0, 0, axis_index_groups=groups, tiled=True)


def pass_on(block, step, turn):
    count = lax.axis_size("expert")
    route = []
    for i in range(count):
        place = i % SPLIT // 2
        came = place - step * (turn - 1)
        if 0 <= came < QUADS and 0 <= place + step < QUADS:
            route.append((i, i + 2 * step))
    return lax.ppermute(block, "expert", route)


def neighbour(block):
    count = lax.axis_size("expert")
    return lax.ppermute(block, "expert", [(i, i ^ 1) for i in range(count)])


def swap(block, distance):
    count = lax.axis_size("expert")
    return lax.ppermute(block, "expert", [(i, i ^ 2 * distance) for i in range(count)])


def reduce_groups(pipes, count):
    half = pipes // 2
    return [
        [(p + half * h) * count + i + side for h in range(2) for side in range(2)]
        for p in range(half)
        for i in range(0, count, 2)
    ]


def dot(a, b, dims=((1,), (0,))):
    return lax.dot_general(a, b, (dims, ((), ())), preferred_element_type=F32)


def kernel_call(body, out_shape, flops, moved, scalars=0, **kwargs):
    def call(*operands):
        specs = [pl.BlockSpec(memory_space=pltpu.SMEM)] * scalars
        specs += [pl.BlockSpec(memory_space=pltpu.VMEM)] * (len(operands) - scalars)
        return pl.pallas_call(
            body,
            out_shape=out_shape,
            in_specs=specs,
            out_specs=jax.tree.map(lambda _: pl.BlockSpec(memory_space=pltpu.VMEM), out_shape),
            compiler_params=pltpu.CompilerParams(vmem_limit_bytes=VMEM_LIMIT),
            cost_estimate=pl.CostEstimate(flops=flops, bytes_accessed=moved, transcendentals=0),
            **kwargs,
        )(*operands)

    return call


def relay_kernel(quad_ref, w_ref, *rest):
    outs, turned = rest[:-1], rest[-1]
    quad = quad_ref[0]
    turned[...] = w_ref[...].T
    eighth = outs[0].shape[0] // 2
    for d, out in enumerate(outs):
        for h in range(2):
            start = pl.multiple_of((h * QUADS + (quad ^ d)) * eighth, 16)
            out[h * eighth : (h + 1) * eighth, :] = turned[pl.ds(start, eighth), :]


def gather_kernel(window, ids_ref, gates_ref, tok_ref, picked_ref, spread_ref):
    slots, toks = window * CAP, tok_ref.shape[0]
    slot = lax.broadcasted_iota(jnp.int32, (slots, toks), 0)
    expert, nth = slot // CAP, slot % CAP
    weight = jnp.zeros((slots, toks), F32)
    member = jnp.zeros((slots, toks), F32)
    for j in range(ids_ref.shape[0]):
        hit = ids_ref[j : j + 1, :] == expert
        weight = weight + jnp.where(hit, gates_ref[j : j + 1, :], 0.0)
        member = jnp.where(hit, 1.0, member)
    before = lax.broadcasted_iota(jnp.int32, (toks, toks), 0)
    after = lax.broadcasted_iota(jnp.int32, (toks, toks), 1)
    upto = jnp.where(before <= after, 1.0, 0.0).astype(BF16)
    ranking = dot(member.astype(BF16), upto)
    matched = (member > 0.5) & (ranking == (nth + 1).astype(F32))
    spread_ref[...] = jnp.where(matched, weight, 0.0)
    selector = jnp.where(matched, 1.0, 0.0).astype(BF16)
    quarter = picked_ref.shape[2]
    for q in range(QUADS):
        rows = dot(selector, tok_ref[:, q * quarter : (q + 1) * quarter]).astype(BF16)
        for k in range(window):
            picked_ref[k * QUADS + q] = rows[k * CAP : (k + 1) * CAP]


def acts_kernel(quad_ref, here, up1, up2, down1, down2, wg, wu, wg2, wu2, acts_ref):
    quad = quad_ref[0]
    quarter, units = here.shape[1], wg.shape[1]
    parts = ((here, None, 0), (up1, None, 1), (down1, None, 3), (up2, down2, 2))
    totals = [None] * 4
    for first, second, distance in parts:
        start = pl.multiple_of((quad + distance) % QUADS * quarter, quarter)
        rows = first[...] if second is None else first[...] + second[...]
        for n, weight in enumerate((wg, wu, wg2, wu2)):
            part = dot(rows, weight[pl.ds(start, quarter), :])
            totals[n] = part if totals[n] is None else totals[n] + part
    for n in range(4):
        acts_ref[:, n * units : (n + 1) * units] = totals[n]


def hidden_kernel(quad_ref, acts, up3, down3, wg, wu, wg2, wu2, hidden_ref):
    quad = quad_ref[0]
    quarter, units = up3.shape[1], wg.shape[1]
    last = jnp.where(quad * 2 < QUADS, QUADS - 1, 0)
    start = pl.multiple_of(last * quarter, quarter)
    rows = up3[...] + down3[...]
    both = []
    for n, weight in enumerate((wg, wu, wg2, wu2)):
        both.append(acts[:, n * units : (n + 1) * units] + dot(rows, weight[pl.ds(start, quarter), :]))
    for side in range(2):
        gate, up = both[2 * side], both[2 * side + 1]
        value = (gate / (1.0 + jnp.exp(-gate)) * up).astype(BF16)
        for s in range(QUADS):
            hidden_ref[s, :, side * units : (side + 1) * units] = value


def down_kernel(quad_ref, hidden, down, down_other, out_ref):
    quad = quad_ref[0]
    total = None
    for d in range(QUADS):
        slab = jnp.concatenate([down[d], down_other[d]], axis=1)
        part = dot(hidden[quad ^ d], slab, ((1,), (1,)))
        total = part if total is None else total + part
    blocks, cap, quarter = out_ref.shape
    out_ref[...] = total.astype(BF16).reshape(blocks, cap, quarter)


def mix_kernel(window, spread_ref, loss_ref, back, mixed_ref, cotan_ref):
    spread = spread_ref[...]
    high = spread.astype(BF16)
    rest = spread - high.astype(F32)
    middle = rest.astype(BF16)
    low = (rest - middle.astype(F32)).astype(BF16)
    weights = jnp.concatenate([high, middle, low], axis=0)
    chosen = jnp.where(spread > 0.0, 1.0, 0.0).astype(BF16)
    scale = jnp.sum(spread * loss_ref[...], axis=1, keepdims=True)
    eighth = back.shape[2] // 2
    halves = [[], []]
    for q in range(QUADS):
        rows = jnp.concatenate([back[k * QUADS + q] for k in range(window)], axis=0)
        rows = jnp.concatenate([rows, rows, rows], axis=0)
        mixed = dot(weights, rows, ((0,), (0,))).astype(BF16)
        cotan = (scale * dot(chosen, mixed)).astype(BF16)
        for k in range(window):
            cotan_ref[k * QUADS + q] = cotan[k * CAP : (k + 1) * CAP]
        for h in range(2):
            halves[h].append(mixed[:, h * eighth : (h + 1) * eighth])
    mixed_ref[...] = jnp.concatenate(halves[0] + halves[1], axis=1)


def grads_kernel(side_ref, cotan, hidden, grads_ref):
    side = side_ref[0]
    eighth, units = grads_ref.shape[2:]
    for s in range(QUADS):
        part = dot(cotan[...], hidden[s], ((0,), (0,))).astype(BF16)
        for h in range(2):
            for other in range(2):
                grads_ref[2 * h + (side + other) % 2, s] = part[
                    h * eighth : (h + 1) * eighth, other * units : (other + 1) * units
                ]


def per_device(tokens, expert_ids, gates, loss_weight, w_gate, w_up, w_down):
    tok_count, width = tokens.shape[1:]
    units = w_down.shape[1]
    count = lax.axis_size("expert")
    window = count // SPLIT
    quarter, eighth = width // QUADS, width // (2 * QUADS)
    place = lax.axis_index("expert")
    quad = (place % SPLIT // 2).reshape(1)
    side = (place % 2).reshape(1)
    by_column, by_quad = columns(count), quads(count)
    blocks = count // 2
    held = blocks * CAP

    gate_other = neighbour(w_gate[0])
    up_other = neighbour(w_up[0])

    down = kernel_call(
        relay_kernel, (jax.ShapeDtypeStruct((quarter, units), BF16),) * QUADS,
        0, 4 * width * units, 1, scratch_shapes=[pltpu.VMEM((width, units), BF16)],
    )(quad, w_down[0])
    down = jnp.stack([down[0]] + [swap(down[d], d) for d in range(1, QUADS)])

    picked, spread = kernel_call(
        functools.partial(gather_kernel, window),
        (
            jax.ShapeDtypeStruct((window * QUADS, CAP, quarter), BF16),
            jax.ShapeDtypeStruct((window * CAP, tok_count), F32),
        ),
        2 * window * CAP * tok_count * width, 3 * tok_count * width,
    )(expert_ids[0].T, gates[0].T, tokens[0])
    rows = exchange(picked, "expert", by_column).reshape(held, quarter)
    rows, gate_other, up_other, down = lax.optimization_barrier((rows, gate_other, up_other, down))
    down_other = neighbour(down)
    ups, downs = [rows], [rows]
    for turn in range(1, QUADS):
        ups.append(pass_on(ups[-1], 1, turn))
        downs.append(pass_on(downs[-1], -1, turn))
    weights = (w_gate[0], w_up[0], gate_other, up_other)
    acts = kernel_call(
        acts_kernel, jax.ShapeDtypeStruct((held, 4 * units), F32),
        8 * held * width * units, 8 * width * units, 1,
    )(quad, rows, downs[1], downs[2], ups[1], ups[2], *weights)
    hidden = kernel_call(
        hidden_kernel, jax.ShapeDtypeStruct((QUADS, held, 2 * units), BF16),
        2 * held * width * units, 2 * width * units, 1,
    )(quad, acts, downs[3], ups[3], *weights)
    hidden, down_other = lax.optimization_barrier((hidden, down_other))
    hidden = exchange(hidden, "expert", by_quad)
    out = kernel_call(
        down_kernel, jax.ShapeDtypeStruct((blocks, CAP, quarter), BF16),
        4 * held * width * units, 4 * width * units, 1,
    )(quad, hidden, down, down_other)
    back = exchange(out, "expert", by_column)

    output, cotan = kernel_call(
        functools.partial(mix_kernel, window),
        (
            jax.ShapeDtypeStruct((tok_count, width), BF16),
            jax.ShapeDtypeStruct((window * QUADS, CAP, quarter), BF16),
        ),
        8 * window * CAP * tok_count * width, 4 * tok_count * width,
    )(spread, loss_weight, back)
    cotan = exchange(cotan, "expert", by_column).reshape(held, quarter)

    grads = kernel_call(
        grads_kernel, jax.ShapeDtypeStruct((2 * 2, QUADS, eighth, units), BF16),
        4 * held * width * units, 4 * width * units, 1,
    )(side, cotan, hidden)
    groups = reduce_groups(lax.axis_size("pipe"), count)
    parts = exchange(grads, ("pipe", "expert"), groups)
    share = jnp.sum(parts.astype(F32), axis=0).astype(BF16)
    share = exchange(share, "expert", by_quad).reshape(QUADS * eighth, units).T
    return output[None], share[None]


def solution(mesh):
    in_specs = (
        P("pipe", "expert", None),
        P("pipe", "expert", None),
        P("pipe", "expert", None),
        P("pipe", "expert"),
        P("pipe", None, "expert"),
        P("pipe", None, "expert"),
        P("pipe", "expert", None),
    )
    out_specs = (P("pipe", "expert", None), P("pipe", "expert", None))
    return jax.shard_map(
        per_device, mesh=mesh, in_specs=in_specs, out_specs=out_specs, check_vma=False
    )
```

```python
import functools

import jax
import jax.numpy as jnp
from jax import lax
from jax.experimental import pallas as pl
from jax.experimental.pallas import tpu as pltpu
from jax.sharding import PartitionSpec as P

SPLIT = 8
CAP = 16
QUADS = 4
BF16 = jnp.bfloat16
F32 = jnp.float32
VMEM_LIMIT = 48 * 1024 * 1024


def columns(count):
    return [[i for i in range(count) if i % 2 == side] for side in range(2)]


def quads(count):
    return [
        [base + 2 * place + side for place in range(QUADS)]
        for base in range(0, count, SPLIT)
        for side in range(2)
    ]


def exchange(blocks, axis, groups):
    return lax.all_to_all(blocks, axis, 0, 0, axis_index_groups=groups, tiled=True)


def pass_on(block, step, turn):
    count = lax.axis_size("expert")
    route = []
    for i in range(count):
        place = i % SPLIT // 2
        came = place - step * (turn - 1)
        if 0 <= came < QUADS and 0 <= place + step < QUADS:
            route.append((i, i + 2 * step))
    return lax.ppermute(block, "expert", route)


def neighbour(block):
    count = lax.axis_size("expert")
    return lax.ppermute(block, "expert", [(i, i ^ 1) for i in range(count)])


def swap(block, distance):
    count = lax.axis_size("expert")
    return lax.ppermute(block, "expert", [(i, i ^ 2 * distance) for i in range(count)])


def cross(block, flip_side, flip_pipe):
    pipes, count = lax.axis_size("pipe"), lax.axis_size("expert")
    route = []
    for p in range(pipes):
        for i in range(count):
            other = (p + pipes // 2) % pipes if flip_pipe else p
            route.append((p * count + i, other * count + (i ^ 1 if flip_side else i)))
    return lax.ppermute(block, ("pipe", "expert"), route)


def reduce_groups(pipes, count):
    half = pipes // 2
    return [
        [(p + half * h) * count + i + side for h in range(2) for side in range(2)]
        for p in range(half)
        for i in range(0, count, 2)
    ]


def dot(a, b, dims=((1,), (0,))):
    return lax.dot_general(a, b, (dims, ((), ())), preferred_element_type=F32)


def kernel_call(body, out_shape, flops, moved, scalars=0, space=pltpu.VMEM, **kwargs):
    def call(*operands):
        specs = [pl.BlockSpec(memory_space=pltpu.SMEM)] * scalars
        specs += [pl.BlockSpec(memory_space=space)] * (len(operands) - scalars)
        return pl.pallas_call(
            body,
            out_shape=out_shape,
            in_specs=specs,
            out_specs=jax.tree.map(lambda _: pl.BlockSpec(memory_space=pltpu.VMEM), out_shape),
            compiler_params=pltpu.CompilerParams(vmem_limit_bytes=VMEM_LIMIT),
            cost_estimate=pl.CostEstimate(flops=flops, bytes_accessed=moved, transcendentals=0),
            **kwargs,
        )(*operands)

    return call


def quad_of(place_ref):
    return (place_ref[0] & (SPLIT - 1)) >> 1


def relay_kernel(place_ref, w_ref, *rest):
    outs, turned = rest[:-1], rest[-1]
    quad = quad_of(place_ref)
    turned[...] = w_ref[...].T
    eighth = outs[0].shape[0] // 2
    for d, out in enumerate(outs):
        for h in range(2):
            start = pl.multiple_of((h * QUADS + (quad ^ d)) * eighth, 16)
            out[h * eighth : (h + 1) * eighth, :] = turned[pl.ds(start, eighth), :]


def gather_kernel(window, ids, gates, tokens, picked_ref, spread_ref, ids_ref, gates_ref, tok_ref, sems):
    pairs = ((ids, ids_ref), (gates, gates_ref), (tokens, tok_ref))
    copies = [pltpu.make_async_copy(a, b, sems.at[n]) for n, (a, b) in enumerate(pairs)]
    for copy in copies:
        copy.start()
    for copy in copies:
        copy.wait()
    slots, toks = window * CAP, tok_ref.shape[0]
    slot = lax.broadcasted_iota(jnp.int32, (slots, toks), 0)
    expert, nth = slot // CAP, slot % CAP
    weight = jnp.zeros((slots, toks), F32)
    member = jnp.zeros((slots, toks), F32)
    for j in range(ids_ref.shape[0]):
        hit = ids_ref[j : j + 1, :] == expert
        weight = weight + jnp.where(hit, gates_ref[j : j + 1, :], 0.0)
        member = jnp.where(hit, 1.0, member)
    before = lax.broadcasted_iota(jnp.int32, (toks, toks), 0)
    after = lax.broadcasted_iota(jnp.int32, (toks, toks), 1)
    upto = jnp.where(before <= after, 1.0, 0.0).astype(BF16)
    ranking = dot(member.astype(BF16), upto)
    matched = (member > 0.5) & (ranking == (nth + 1).astype(F32))
    spread_ref[...] = jnp.where(matched, weight, 0.0)
    selector = jnp.where(matched, 1.0, 0.0).astype(BF16)
    quarter = picked_ref.shape[2]
    for q in range(QUADS):
        rows = dot(selector, tok_ref[:, q * quarter : (q + 1) * quarter]).astype(BF16)
        for k in range(window):
            picked_ref[k * QUADS + q] = rows[k * CAP : (k + 1) * CAP]


def acts_kernel(place_ref, here, up1, up2, down1, down2, wg, wu, wg2, wu2, acts_ref):
    quad = quad_of(place_ref)
    quarter, units = here.shape[1], wg.shape[1]
    parts = ((here, None, 0), (up1, None, 1), (down1, None, 3), (up2, down2, 2))
    totals = [None] * 4
    for first, second, distance in parts:
        start = pl.multiple_of(((quad + distance) & (QUADS - 1)) * quarter, quarter)
        rows = first[...] if second is None else first[...] + second[...]
        for n, weight in enumerate((wg, wu, wg2, wu2)):
            part = dot(rows, weight[pl.ds(start, quarter), :])
            totals[n] = part if totals[n] is None else totals[n] + part
    for n in range(4):
        acts_ref[:, n * units : (n + 1) * units] = totals[n]


def hidden_kernel(place_ref, acts, up3, down3, wg, wu, wg2, wu2, hidden_ref):
    quad = quad_of(place_ref)
    quarter, units = up3.shape[1], wg.shape[1]
    last = jnp.where(quad * 2 < QUADS, QUADS - 1, 0)
    start = pl.multiple_of(last * quarter, quarter)
    rows = up3[...] + down3[...]
    both = []
    for n, weight in enumerate((wg, wu, wg2, wu2)):
        both.append(acts[:, n * units : (n + 1) * units] + dot(rows, weight[pl.ds(start, quarter), :]))
    for side in range(2):
        gate, up = both[2 * side], both[2 * side + 1]
        value = (gate / (1.0 + jnp.exp(-gate)) * up).astype(BF16)
        for s in range(QUADS):
            hidden_ref[s, :, side * units : (side + 1) * units] = value


def down_kernel(place_ref, hidden, down, down_other, out_ref):
    quad = quad_of(place_ref)
    total = None
    for d in range(QUADS):
        slab = jnp.concatenate([down[d], down_other[d]], axis=1)
        part = dot(hidden[quad ^ d], slab, ((1,), (1,)))
        total = part if total is None else total + part
    blocks, cap, quarter = out_ref.shape
    out_ref[...] = total.astype(BF16).reshape(blocks, cap, quarter)


def mix_kernel(window, spread_ref, loss_ref, back, mixed_ref, cotan_ref):
    spread = spread_ref[...]
    high = spread.astype(BF16)
    rest = spread - high.astype(F32)
    middle = rest.astype(BF16)
    low = (rest - middle.astype(F32)).astype(BF16)
    weights = jnp.concatenate([high, middle, low], axis=0)
    chosen = jnp.where(spread > 0.0, 1.0, 0.0).astype(BF16)
    scale = jnp.sum(spread * loss_ref[...], axis=1, keepdims=True)
    eighth = back.shape[2] // 2
    halves = [[], []]
    for q in range(QUADS):
        rows = jnp.concatenate([back[k * QUADS + q] for k in range(window)], axis=0)
        rows = jnp.concatenate([rows, rows, rows], axis=0)
        mixed = dot(weights, rows, ((0,), (0,))).astype(BF16)
        cotan = (scale * dot(chosen, mixed)).astype(BF16)
        for k in range(window):
            cotan_ref[k * QUADS + q] = cotan[k * CAP : (k + 1) * CAP]
        for h in range(2):
            halves[h].append(mixed[:, h * eighth : (h + 1) * eighth])
    mixed_ref[...] = jnp.concatenate(halves[0] + halves[1], axis=1)


def turn_kernel(cotan, out_ref):
    turned = cotan[...].T
    eighth = out_ref.shape[1]
    for h in range(2):
        for side in range(2):
            out_ref[2 * h + side] = turned[h * eighth : (h + 1) * eighth, :]


def grads_kernel(place_ref, cotans, own, across, mirrored, opposite, grads_ref):
    mine = 2 * place_ref[1] + (place_ref[0] & 1)
    units = own.shape[2]
    total = None
    for flip, hidden in enumerate((own, across, mirrored, opposite)):
        slab = jnp.concatenate([hidden[s] for s in range(QUADS)], axis=1)
        part = dot(cotans[mine ^ flip], slab)
        total = part if total is None else total + part
    for s in range(QUADS):
        grads_ref[s] = total[:, s * units : (s + 1) * units].astype(BF16)


def per_device(tokens, expert_ids, gates, loss_weight, w_gate, w_up, w_down):
    tok_count, width = tokens.shape[1:]
    choices = gates.shape[2]
    units = w_down.shape[1]
    count = lax.axis_size("expert")
    window = count // SPLIT
    quarter, eighth = width // QUADS, width // (2 * QUADS)
    place = lax.axis_index("expert")
    mirror = lax.axis_index("pipe") // (lax.axis_size("pipe") // 2)
    place = jnp.stack([place, mirror])
    by_column, by_quad = columns(count), quads(count)
    blocks = count // 2
    held = blocks * CAP

    gate_other = neighbour(w_gate[0])
    up_other = neighbour(w_up[0])

    down = kernel_call(
        relay_kernel, (jax.ShapeDtypeStruct((quarter, units), BF16),) * QUADS,
        0, 4 * width * units, 1, scratch_shapes=[pltpu.VMEM((width, units), BF16)],
    )(place, w_down[0])
    down = [down[0]] + [swap(down[d], d) for d in range(1, QUADS)]

    picked, spread = kernel_call(
        functools.partial(gather_kernel, window),
        (
            jax.ShapeDtypeStruct((window * QUADS, CAP, quarter), BF16),
            jax.ShapeDtypeStruct((window * CAP, tok_count), F32),
        ),
        2 * window * CAP * tok_count * width, 3 * tok_count * width, space=pl.ANY,
        scratch_shapes=[
            pltpu.VMEM((choices, tok_count), jnp.int32),
            pltpu.VMEM((choices, tok_count), F32),
            pltpu.VMEM((tok_count, width), BF16),
            pltpu.SemaphoreType.DMA((3,)),
        ],
    )(expert_ids[0].T, gates[0].T, tokens[0])
    once = lax.optimization_barrier(jnp.int32(1))
    rows = lax.fori_loop(0, once, lambda _, blocks: exchange(blocks, "expert", by_column), picked)
    rows = rows.reshape(held, quarter)
    rows, gate_other, up_other, *down = lax.optimization_barrier((rows, gate_other, up_other, *down))
    down = jnp.stack(down)
    down_other = neighbour(down)
    ups, downs = [rows], [rows]
    for turn in range(1, QUADS):
        ups.append(pass_on(ups[-1], 1, turn))
        downs.append(pass_on(downs[-1], -1, turn))
    weights = (w_gate[0], w_up[0], gate_other, up_other)
    acts = kernel_call(
        acts_kernel, jax.ShapeDtypeStruct((held, 4 * units), F32),
        8 * held * width * units, 8 * width * units, 1,
    )(place, rows, downs[1], downs[2], ups[1], ups[2], *weights)
    hidden = kernel_call(
        hidden_kernel, jax.ShapeDtypeStruct((QUADS, held, 2 * units), BF16),
        2 * held * width * units, 2 * width * units, 1,
    )(place, acts, downs[3], ups[3], *weights)
    hidden, down_other = lax.optimization_barrier((hidden, down_other))
    hidden = exchange(hidden, "expert", by_quad)
    out = kernel_call(
        down_kernel, jax.ShapeDtypeStruct((blocks, CAP, quarter), BF16),
        4 * held * width * units, 4 * width * units, 1,
    )(place, hidden, down, down_other)
    back = exchange(out, "expert", by_column)
    own, other = hidden[:, :, :units], hidden[:, :, units:]
    across, mirrored, opposite = cross(other, 1, 0), cross(own, 0, 1), cross(other, 1, 1)
    back, across, mirrored, opposite = lax.optimization_barrier((back, across, mirrored, opposite))

    output, cotan = kernel_call(
        functools.partial(mix_kernel, window),
        (
            jax.ShapeDtypeStruct((tok_count, width), BF16),
            jax.ShapeDtypeStruct((window * QUADS, CAP, quarter), BF16),
        ),
        8 * window * CAP * tok_count * width, 4 * tok_count * width,
    )(spread, loss_weight, back)
    cotan = exchange(cotan, "expert", by_column).reshape(held, quarter)

    groups = reduce_groups(lax.axis_size("pipe"), count)
    cotan = kernel_call(
        turn_kernel, jax.ShapeDtypeStruct((2 * 2, eighth, held), BF16), 0, 6 * held * quarter
    )(cotan)
    cotan = exchange(cotan, ("pipe", "expert"), groups)
    share = kernel_call(
        grads_kernel, jax.ShapeDtypeStruct((QUADS, eighth, units), BF16),
        4 * held * width * units, 4 * width * units, 1,
    )(place, cotan, own, across, mirrored, opposite)
    share = exchange(share, "expert", by_quad).reshape(QUADS * eighth, units).T
    return output[None], share[None]


def solution(mesh):
    in_specs = (
        P("pipe", "expert", None),
        P("pipe", "expert", None),
        P("pipe", "expert", None),
        P("pipe", "expert"),
        P("pipe", None, "expert"),
        P("pipe", None, "expert"),
        P("pipe", "expert", None),
    )
    out_specs = (P("pipe", "expert", None), P("pipe", "expert", None))
    return jax.shard_map(
        per_device, mesh=mesh, in_specs=in_specs, out_specs=out_specs, check_vma=False
    )
```

```python
import functools

import jax
import jax.numpy as jnp
from jax import lax
from jax.experimental import pallas as pl
from jax.experimental.pallas import tpu as pltpu
from jax.sharding import PartitionSpec as P

SPLIT = 8
CAP = 16
QUADS = 4
BF16 = jnp.bfloat16
F32 = jnp.float32
VMEM_LIMIT = 20 * 1024 * 1024


def columns(count):
    return [[i for i in range(count) if i % 2 == side] for side in range(2)]


def quads(count):
    return [
        [base + 2 * place + side for place in range(QUADS)]
        for base in range(0, count, SPLIT)
        for side in range(2)
    ]


def exchange(blocks, axis, groups):
    return lax.all_to_all(blocks, axis, 0, 0, axis_index_groups=groups, tiled=True)


def pass_on(block, step, turn):
    count = lax.axis_size("expert")
    route = []
    for i in range(count):
        place = i % SPLIT // 2
        came = place - step * (turn - 1)
        if 0 <= came < QUADS and 0 <= place + step < QUADS:
            route.append((i, i + 2 * step))
    return lax.ppermute(block, "expert", route)


def neighbour(block):
    count = lax.axis_size("expert")
    return lax.ppermute(block, "expert", [(i, i ^ 1) for i in range(count)])


def swap(block, distance):
    count = lax.axis_size("expert")
    return lax.ppermute(block, "expert", [(i, i ^ 2 * distance) for i in range(count)])


def cross(block, flip_side, flip_pipe):
    pipes, count = lax.axis_size("pipe"), lax.axis_size("expert")
    route = []
    for p in range(pipes):
        for i in range(count):
            other = (p + pipes // 2) % pipes if flip_pipe else p
            route.append((p * count + i, other * count + (i ^ 1 if flip_side else i)))
    return lax.ppermute(block, ("pipe", "expert"), route)


def reduce_groups(pipes, count):
    half = pipes // 2
    return [
        [(p + half * h) * count + i + side for h in range(2) for side in range(2)]
        for p in range(half)
        for i in range(0, count, 2)
    ]


def dot(a, b, dims=((1,), (0,))):
    return lax.dot_general(a, b, (dims, ((), ())), preferred_element_type=F32)


def kernel_call(body, out_shape, flops, moved, scalars=0, space=pltpu.VMEM, **kwargs):
    def call(*operands):
        specs = [pl.BlockSpec(memory_space=pltpu.SMEM)] * scalars
        specs += [pl.BlockSpec(memory_space=space)] * (len(operands) - scalars)
        return pl.pallas_call(
            body,
            out_shape=out_shape,
            in_specs=specs,
            out_specs=jax.tree.map(lambda _: pl.BlockSpec(memory_space=pltpu.VMEM), out_shape),
            compiler_params=pltpu.CompilerParams(vmem_limit_bytes=VMEM_LIMIT),
            cost_estimate=pl.CostEstimate(flops=flops, bytes_accessed=moved, transcendentals=0),
            **kwargs,
        )(*operands)

    return call


def quad_of(place_ref):
    return (place_ref[0] & (SPLIT - 1)) >> 1


def relay_kernel(place_ref, w_ref, *rest):
    outs, turned = rest[:-1], rest[-1]
    quad = quad_of(place_ref)
    turned[...] = w_ref[...].T
    eighth = outs[0].shape[0] // 2
    for d, out in enumerate(outs):
        for h in range(2):
            start = pl.multiple_of((h * QUADS + (quad ^ d)) * eighth, 16)
            out[h * eighth : (h + 1) * eighth, :] = turned[pl.ds(start, eighth), :]


def gather_kernel(window, ids, gates, tokens, picked_ref, spread_ref, ids_ref, gates_ref, tok_ref, sems):
    pairs = ((ids, ids_ref), (gates, gates_ref), (tokens, tok_ref))
    copies = [pltpu.make_async_copy(a, b, sems.at[n]) for n, (a, b) in enumerate(pairs)]
    for copy in copies:
        copy.start()
    for copy in copies:
        copy.wait()
    slots, toks = window * CAP, tok_ref.shape[0]
    slot = lax.broadcasted_iota(jnp.int32, (slots, toks), 0)
    expert, nth = slot // CAP, slot % CAP
    weight = jnp.zeros((slots, toks), F32)
    member = jnp.zeros((slots, toks), F32)
    for j in range(ids_ref.shape[0]):
        hit = ids_ref[j : j + 1, :] == expert
        weight = weight + jnp.where(hit, gates_ref[j : j + 1, :], 0.0)
        member = jnp.where(hit, 1.0, member)
    before = lax.broadcasted_iota(jnp.int32, (toks, toks), 0)
    after = lax.broadcasted_iota(jnp.int32, (toks, toks), 1)
    upto = jnp.where(before <= after, 1.0, 0.0).astype(BF16)
    ranking = dot(member.astype(BF16), upto)
    matched = (member > 0.5) & (ranking == (nth + 1).astype(F32))
    spread_ref[...] = jnp.where(matched, weight, 0.0)
    selector = jnp.where(matched, 1.0, 0.0).astype(BF16)
    quarter = picked_ref.shape[2]
    for q in range(QUADS):
        rows = dot(selector, tok_ref[:, q * quarter : (q + 1) * quarter]).astype(BF16)
        for k in range(window):
            picked_ref[k * QUADS + q] = rows[k * CAP : (k + 1) * CAP]


def acts_kernel(place_ref, here, up1, up2, down1, down2, wg, wu, wg2, wu2, acts_ref):
    quad = quad_of(place_ref)
    quarter, units = here.shape[1], wg.shape[1]
    parts = ((here, None, 0), (up1, None, 1), (down1, None, 3), (up2, down2, 2))
    totals = [None] * 4
    for first, second, distance in parts:
        start = pl.multiple_of(((quad + distance) & (QUADS - 1)) * quarter, quarter)
        rows = first[...] if second is None else first[...] + second[...]
        for n, weight in enumerate((wg, wu, wg2, wu2)):
            part = dot(rows, weight[pl.ds(start, quarter), :])
            totals[n] = part if totals[n] is None else totals[n] + part
    for n in range(4):
        acts_ref[:, n * units : (n + 1) * units] = totals[n]


def hidden_kernel(place_ref, acts, up3, down3, wg, wu, wg2, wu2, hidden_ref):
    quad = quad_of(place_ref)
    quarter, units = up3.shape[1], wg.shape[1]
    last = jnp.where(quad * 2 < QUADS, QUADS - 1, 0)
    start = pl.multiple_of(last * quarter, quarter)
    rows = up3[...] + down3[...]
    both = []
    for n, weight in enumerate((wg, wu, wg2, wu2)):
        both.append(acts[:, n * units : (n + 1) * units] + dot(rows, weight[pl.ds(start, quarter), :]))
    for side in range(2):
        gate, up = both[2 * side], both[2 * side + 1]
        value = (gate / (1.0 + jnp.exp(-gate)) * up).astype(BF16)
        for s in range(QUADS):
            hidden_ref[s, :, side * units : (side + 1) * units] = value


def down_kernel(place_ref, hidden, down, down_other, out_ref):
    quad = quad_of(place_ref)
    total = None
    for d in range(QUADS):
        slab = jnp.concatenate([down[d], down_other[d]], axis=1)
        part = dot(hidden[quad ^ d], slab, ((1,), (1,)))
        total = part if total is None else total + part
    blocks, cap, quarter = out_ref.shape
    out_ref[...] = total.astype(BF16).reshape(blocks, cap, quarter)


def mix_kernel(window, spread_ref, loss_ref, back, mixed_ref, cotan_ref):
    spread = spread_ref[...]
    high = spread.astype(BF16)
    rest = spread - high.astype(F32)
    middle = rest.astype(BF16)
    low = (rest - middle.astype(F32)).astype(BF16)
    weights = jnp.concatenate([high, middle, low], axis=0)
    chosen = jnp.where(spread > 0.0, 1.0, 0.0).astype(BF16)
    scale = jnp.sum(spread * loss_ref[...], axis=1, keepdims=True)
    eighth = back.shape[2] // 2
    halves = [[], []]
    for q in range(QUADS):
        rows = jnp.concatenate([back[k * QUADS + q] for k in range(window)], axis=0)
        rows = jnp.concatenate([rows, rows, rows], axis=0)
        mixed = dot(weights, rows, ((0,), (0,))).astype(BF16)
        cotan = (scale * dot(chosen, mixed)).astype(BF16)
        for k in range(window):
            cotan_ref[k * QUADS + q] = cotan[k * CAP : (k + 1) * CAP]
        for h in range(2):
            halves[h].append(mixed[:, h * eighth : (h + 1) * eighth])
    mixed_ref[...] = jnp.concatenate(halves[0] + halves[1], axis=1)


def turn_kernel(cotan, out_ref):
    turned = cotan[...].T
    eighth = out_ref.shape[1]
    for h in range(2):
        for side in range(2):
            out_ref[2 * h + side] = turned[h * eighth : (h + 1) * eighth, :]


def grads_kernel(place_ref, cotans, own, across, mirrored, opposite, grads_ref):
    mine = 2 * place_ref[1] + (place_ref[0] & 1)
    units = own.shape[2]
    total = None
    for flip, hidden in enumerate((own, across, mirrored, opposite)):
        slab = jnp.concatenate([hidden[s] for s in range(QUADS)], axis=1)
        part = dot(cotans[mine ^ flip], slab)
        total = part if total is None else total + part
    for s in range(QUADS):
        grads_ref[s] = total[:, s * units : (s + 1) * units].astype(BF16)


def per_device(tokens, expert_ids, gates, loss_weight, w_gate, w_up, w_down):
    tok_count, width = tokens.shape[1:]
    choices = gates.shape[2]
    units = w_down.shape[1]
    count = lax.axis_size("expert")
    window = count // SPLIT
    quarter, eighth = width // QUADS, width // (2 * QUADS)
    place = lax.axis_index("expert")
    mirror = lax.axis_index("pipe") // (lax.axis_size("pipe") // 2)
    place = jnp.stack([place, mirror])
    by_column, by_quad = columns(count), quads(count)
    blocks = count // 2
    held = blocks * CAP

    gate_other = neighbour(w_gate[0])
    up_other = neighbour(w_up[0])

    down = kernel_call(
        relay_kernel, (jax.ShapeDtypeStruct((quarter, units), BF16),) * QUADS,
        0, 4 * width * units, 1, scratch_shapes=[pltpu.VMEM((width, units), BF16)],
    )(place, w_down[0])
    down = [down[0]] + [swap(down[d], d) for d in range(1, QUADS)]

    picked, spread = kernel_call(
        functools.partial(gather_kernel, window),
        (
            jax.ShapeDtypeStruct((window * QUADS, CAP, quarter), BF16),
            jax.ShapeDtypeStruct((window * CAP, tok_count), F32),
        ),
        2 * window * CAP * tok_count * width, 3 * tok_count * width, space=pl.ANY,
        scratch_shapes=[
            pltpu.VMEM((choices, tok_count), jnp.int32),
            pltpu.VMEM((choices, tok_count), F32),
            pltpu.VMEM((tok_count, width), BF16),
            pltpu.SemaphoreType.DMA((3,)),
        ],
    )(expert_ids[0].T, gates[0].T, tokens[0])
    once = lax.optimization_barrier(jnp.int32(1))
    rows = lax.cond(once > 0, lambda b: exchange(b, "expert", by_column), lambda b: b, picked)
    rows = rows.reshape(held, quarter)
    rows, gate_other, up_other, *down = lax.optimization_barrier((rows, gate_other, up_other, *down))
    down = jnp.stack(down)
    down_other = neighbour(down)
    ups, downs = [rows], [rows]
    for turn in range(1, QUADS):
        ups.append(pass_on(ups[-1], 1, turn))
        downs.append(pass_on(downs[-1], -1, turn))
    weights = (w_gate[0], w_up[0], gate_other, up_other)
    acts = kernel_call(
        acts_kernel, jax.ShapeDtypeStruct((held, 4 * units), F32),
        8 * held * width * units, 8 * width * units, 1,
    )(place, rows, downs[1], downs[2], ups[1], ups[2], *weights)
    hidden = kernel_call(
        hidden_kernel, jax.ShapeDtypeStruct((QUADS, held, 2 * units), BF16),
        2 * held * width * units, 2 * width * units, 1,
    )(place, acts, downs[3], ups[3], *weights)
    hidden, down_other = lax.optimization_barrier((hidden, down_other))
    hidden = exchange(hidden, "expert", by_quad)
    out = kernel_call(
        down_kernel, jax.ShapeDtypeStruct((blocks, CAP, quarter), BF16),
        4 * held * width * units, 4 * width * units, 1,
    )(place, hidden, down, down_other)
    back = exchange(out, "expert", by_column)
    own, other = hidden[:, :, :units], hidden[:, :, units:]
    across, mirrored, opposite = cross(other, 1, 0), cross(own, 0, 1), cross(other, 1, 1)
    back, across, mirrored, opposite = lax.optimization_barrier((back, across, mirrored, opposite))

    output, cotan = kernel_call(
        functools.partial(mix_kernel, window),
        (
            jax.ShapeDtypeStruct((tok_count, width), BF16),
            jax.ShapeDtypeStruct((window * QUADS, CAP, quarter), BF16),
        ),
        8 * window * CAP * tok_count * width, 4 * tok_count * width,
    )(spread, loss_weight, back)
    cotan = exchange(cotan, "expert", by_column).reshape(held, quarter)

    groups = reduce_groups(lax.axis_size("pipe"), count)
    cotan = kernel_call(
        turn_kernel, jax.ShapeDtypeStruct((2 * 2, eighth, held), BF16), 0, 6 * held * quarter
    )(cotan)
    cotan = exchange(cotan, ("pipe", "expert"), groups)
    share = kernel_call(
        grads_kernel, jax.ShapeDtypeStruct((QUADS, eighth, units), BF16),
        4 * held * width * units, 4 * width * units, 1,
    )(place, cotan, own, across, mirrored, opposite)
    share = exchange(share, "expert", by_quad).reshape(QUADS * eighth, units).T
    return output[None], share[None]


def solution(mesh):
    in_specs = (
        P("pipe", "expert", None),
        P("pipe", "expert", None),
        P("pipe", "expert", None),
        P("pipe", "expert"),
        P("pipe", None, "expert"),
        P("pipe", None, "expert"),
        P("pipe", "expert", None),
    )
    out_specs = (P("pipe", "expert", None), P("pipe", "expert", None))
    return jax.shard_map(
        per_device, mesh=mesh, in_specs=in_specs, out_specs=out_specs, check_vma=False
    )
```

```python
import functools

import jax
import jax.numpy as jnp
from jax import lax
from jax.experimental import pallas as pl
from jax.experimental.pallas import tpu as pltpu
from jax.sharding import PartitionSpec as P

SPLIT = 8
CAP = 16
QUADS = 4
BF16 = jnp.bfloat16
F32 = jnp.float32
VMEM_LIMIT = 20 * 1024 * 1024


def columns(count):
    return [[i for i in range(count) if i % 2 == side] for side in range(2)]


def quads(count):
    return [
        [base + 2 * place + side for place in range(QUADS)]
        for base in range(0, count, SPLIT)
        for side in range(2)
    ]


def exchange(blocks, axis, groups):
    return lax.all_to_all(blocks, axis, 0, 0, axis_index_groups=groups, tiled=True)


def pass_on(block, step, turn):
    count = lax.axis_size("expert")
    route = []
    for i in range(count):
        place = i % SPLIT // 2
        came = place - step * (turn - 1)
        if 0 <= came < QUADS and 0 <= place + step < QUADS:
            route.append((i, i + 2 * step))
    return lax.ppermute(block, "expert", route)


def neighbour(block):
    count = lax.axis_size("expert")
    return lax.ppermute(block, "expert", [(i, i ^ 1) for i in range(count)])


def swap(block, distance):
    count = lax.axis_size("expert")
    return lax.ppermute(block, "expert", [(i, i ^ 2 * distance) for i in range(count)])


def cross(block, flip_side, flip_pipe):
    pipes, count = lax.axis_size("pipe"), lax.axis_size("expert")
    route = []
    for p in range(pipes):
        for i in range(count):
            other = (p + pipes // 2) % pipes if flip_pipe else p
            route.append((p * count + i, other * count + (i ^ 1 if flip_side else i)))
    return lax.ppermute(block, ("pipe", "expert"), route)


def reduce_groups(pipes, count):
    half = pipes // 2
    return [
        [(p + half * h) * count + i + side for h in range(2) for side in range(2)]
        for p in range(half)
        for i in range(0, count, 2)
    ]


def dot(a, b, dims=((1,), (0,))):
    return lax.dot_general(a, b, (dims, ((), ())), preferred_element_type=F32)


def kernel_call(body, out_shape, flops, moved, scalars=0, left=0, vmem=VMEM_LIMIT, **kwargs):
    def call(*operands):
        specs = [pl.BlockSpec(memory_space=pltpu.SMEM)] * scalars
        specs += [pl.BlockSpec(memory_space=pltpu.VMEM)] * (len(operands) - scalars - left)
        specs += [pl.BlockSpec(memory_space=pl.ANY)] * left
        return pl.pallas_call(
            body,
            out_shape=out_shape,
            in_specs=specs,
            out_specs=jax.tree.map(lambda _: pl.BlockSpec(memory_space=pltpu.VMEM), out_shape),
            compiler_params=pltpu.CompilerParams(vmem_limit_bytes=vmem),
            cost_estimate=pl.CostEstimate(flops=flops, bytes_accessed=moved, transcendentals=0),
            **kwargs,
        )(*operands)

    return call


def quad_of(place_ref):
    return (place_ref[0] & (SPLIT - 1)) >> 1


def relay_kernel(place_ref, w_ref, gate_ref, up_ref, *rest):
    *outs, pair_ref, turned, sems = rest
    copies = [
        pltpu.make_async_copy(a, pair_ref.at[n], sems.at[n]) for n, a in enumerate((gate_ref, up_ref))
    ]
    for copy in copies:
        copy.start()
    quad = quad_of(place_ref)
    turned[...] = w_ref[...].T
    eighth = outs[0].shape[0] // 2
    for d, out in enumerate(outs):
        for h in range(2):
            start = pl.multiple_of((h * QUADS + (quad ^ d)) * eighth, 16)
            out[h * eighth : (h + 1) * eighth, :] = turned[pl.ds(start, eighth), :]
    for copy in copies:
        copy.wait()


def gather_kernel(window, ids, gates, tokens, picked_ref, spread_ref, ids_ref, gates_ref, tok_ref, sems):
    pairs = ((ids, ids_ref), (gates, gates_ref), (tokens, tok_ref))
    copies = [pltpu.make_async_copy(a, b, sems.at[n]) for n, (a, b) in enumerate(pairs)]
    for copy in copies:
        copy.start()
    for copy in copies:
        copy.wait()
    slots, toks = window * CAP, tok_ref.shape[0]
    slot = lax.broadcasted_iota(jnp.int32, (slots, toks), 0)
    expert, nth = slot // CAP, slot % CAP
    weight = jnp.zeros((slots, toks), F32)
    member = jnp.zeros((slots, toks), F32)
    for j in range(ids_ref.shape[0]):
        hit = ids_ref[j : j + 1, :] == expert
        weight = weight + jnp.where(hit, gates_ref[j : j + 1, :], 0.0)
        member = jnp.where(hit, 1.0, member)
    before = lax.broadcasted_iota(jnp.int32, (toks, toks), 0)
    after = lax.broadcasted_iota(jnp.int32, (toks, toks), 1)
    upto = jnp.where(before <= after, 1.0, 0.0).astype(BF16)
    ranking = dot(member.astype(BF16), upto)
    matched = (member > 0.5) & (ranking == (nth + 1).astype(F32))
    spread_ref[...] = jnp.where(matched, weight, 0.0)
    selector = jnp.where(matched, 1.0, 0.0).astype(BF16)
    quarter = picked_ref.shape[2]
    for q in range(QUADS):
        rows = dot(selector, tok_ref[:, q * quarter : (q + 1) * quarter]).astype(BF16)
        for k in range(window):
            picked_ref[k * QUADS + q] = rows[k * CAP : (k + 1) * CAP]


def acts_kernel(place_ref, here, up1, up2, down1, down2, wg, wu, others, acts_ref):
    quad = quad_of(place_ref)
    quarter, units = here.shape[1], wg.shape[1]
    parts = ((here, None, 0), (up1, None, 1), (down1, None, 3), (up2, down2, 2))
    totals = [None] * 4
    for first, second, distance in parts:
        start = pl.multiple_of(((quad + distance) & (QUADS - 1)) * quarter, quarter)
        rows = first[...] if second is None else first[...] + second[...]
        for n, weight in enumerate((wg, wu, others.at[0], others.at[1])):
            part = dot(rows, weight[pl.ds(start, quarter), :])
            totals[n] = part if totals[n] is None else totals[n] + part
    for n in range(4):
        acts_ref[:, n * units : (n + 1) * units] = totals[n]


def hidden_kernel(place_ref, acts, up3, down3, wg, wu, others, hidden_ref):
    quad = quad_of(place_ref)
    quarter, units = up3.shape[1], wg.shape[1]
    last = jnp.where(quad * 2 < QUADS, QUADS - 1, 0)
    start = pl.multiple_of(last * quarter, quarter)
    rows = up3[...] + down3[...]
    both = []
    for n, weight in enumerate((wg, wu, others.at[0], others.at[1])):
        both.append(acts[:, n * units : (n + 1) * units] + dot(rows, weight[pl.ds(start, quarter), :]))
    for side in range(2):
        gate, up = both[2 * side], both[2 * side + 1]
        value = (gate / (1.0 + jnp.exp(-gate)) * up).astype(BF16)
        for s in range(QUADS):
            hidden_ref[s, :, side * units : (side + 1) * units] = value


def down_kernel(place_ref, hidden, down, down_other, out_ref):
    quad = quad_of(place_ref)
    total = None
    for d in range(QUADS):
        slab = jnp.concatenate([down[d], down_other[d]], axis=1)
        part = dot(hidden[quad ^ d], slab, ((1,), (1,)))
        total = part if total is None else total + part
    blocks, cap, quarter = out_ref.shape
    out_ref[...] = total.astype(BF16).reshape(blocks, cap, quarter)


def mix_kernel(window, spread_ref, loss_ref, back, mixed_ref, cotan_ref):
    spread = spread_ref[...]
    high = spread.astype(BF16)
    rest = spread - high.astype(F32)
    middle = rest.astype(BF16)
    low = (rest - middle.astype(F32)).astype(BF16)
    weights = jnp.concatenate([high, middle, low], axis=0)
    chosen = jnp.where(spread > 0.0, 1.0, 0.0).astype(BF16)
    scale = jnp.sum(spread * loss_ref[...], axis=1, keepdims=True)
    eighth = back.shape[2] // 2
    halves = [[], []]
    for q in range(QUADS):
        rows = jnp.concatenate([back[k * QUADS + q] for k in range(window)], axis=0)
        rows = jnp.concatenate([rows, rows, rows], axis=0)
        mixed = dot(weights, rows, ((0,), (0,))).astype(BF16)
        cotan = (scale * dot(chosen, mixed)).astype(BF16)
        for k in range(window):
            cotan_ref[k * QUADS + q] = cotan[k * CAP : (k + 1) * CAP]
        for h in range(2):
            halves[h].append(mixed[:, h * eighth : (h + 1) * eighth])
    mixed_ref[...] = jnp.concatenate(halves[0] + halves[1], axis=1)


def turn_kernel(cotan, out_ref):
    turned = cotan[...].T
    eighth = out_ref.shape[1]
    for h in range(2):
        for side in range(2):
            out_ref[2 * h + side] = turned[h * eighth : (h + 1) * eighth, :]


def grads_kernel(place_ref, cotans, own, across, mirrored, opposite, grads_ref):
    mine = 2 * place_ref[1] + (place_ref[0] & 1)
    units = own.shape[2]
    total = None
    for flip, hidden in enumerate((own, across, mirrored, opposite)):
        slab = jnp.concatenate([hidden[s] for s in range(QUADS)], axis=1)
        part = dot(cotans[mine ^ flip], slab)
        total = part if total is None else total + part
    for s in range(QUADS):
        grads_ref[s] = total[:, s * units : (s + 1) * units].astype(BF16)


def per_device(tokens, expert_ids, gates, loss_weight, w_gate, w_up, w_down):
    tok_count, width = tokens.shape[1:]
    choices = gates.shape[2]
    units = w_down.shape[1]
    count = lax.axis_size("expert")
    window = count // SPLIT
    quarter, eighth = width // QUADS, width // (2 * QUADS)
    place = lax.axis_index("expert")
    mirror = lax.axis_index("pipe") // (lax.axis_size("pipe") // 2)
    place = jnp.stack([place, mirror])
    by_column, by_quad = columns(count), quads(count)
    blocks = count // 2
    held = blocks * CAP

    *down, gate_up = kernel_call(
        relay_kernel,
        (jax.ShapeDtypeStruct((quarter, units), BF16),) * QUADS
        + (jax.ShapeDtypeStruct((2, width, units), BF16),),
        0, 12 * width * units, 1, left=2, vmem=3 * VMEM_LIMIT,
        scratch_shapes=[pltpu.VMEM((width, units), BF16), pltpu.SemaphoreType.DMA((2,))],
    )(place, w_down[0], w_gate[0], w_up[0])
    others = neighbour(gate_up)
    down = [down[0]] + [swap(down[d], d) for d in range(1, QUADS)]

    picked, spread = kernel_call(
        functools.partial(gather_kernel, window),
        (
            jax.ShapeDtypeStruct((window * QUADS, CAP, quarter), BF16),
            jax.ShapeDtypeStruct((window * CAP, tok_count), F32),
        ),
        2 * window * CAP * tok_count * width, 3 * tok_count * width, left=3,
        scratch_shapes=[
            pltpu.VMEM((choices, tok_count), jnp.int32),
            pltpu.VMEM((choices, tok_count), F32),
            pltpu.VMEM((tok_count, width), BF16),
            pltpu.SemaphoreType.DMA((3,)),
        ],
    )(expert_ids[0].T, gates[0].T, tokens[0])
    once = lax.optimization_barrier(jnp.int32(1))
    rows = lax.cond(once > 0, lambda b: exchange(b, "expert", by_column), lambda b: b, picked)
    rows = rows.reshape(held, quarter)
    rows, others, *down = lax.optimization_barrier((rows, others, *down))
    down = jnp.stack(down)
    down_other = neighbour(down)
    ups, downs = [rows], [rows]
    for turn in range(1, QUADS):
        ups.append(pass_on(ups[-1], 1, turn))
        downs.append(pass_on(downs[-1], -1, turn))
    weights = (w_gate[0], w_up[0], others)
    acts = kernel_call(
        acts_kernel, jax.ShapeDtypeStruct((held, 4 * units), F32),
        8 * held * width * units, 8 * width * units, 1,
    )(place, rows, downs[1], downs[2], ups[1], ups[2], *weights)
    hidden = kernel_call(
        hidden_kernel, jax.ShapeDtypeStruct((QUADS, held, 2 * units), BF16),
        2 * held * width * units, 2 * width * units, 1,
    )(place, acts, downs[3], ups[3], *weights)
    hidden, down_other = lax.optimization_barrier((hidden, down_other))
    hidden = exchange(hidden, "expert", by_quad)
    out = kernel_call(
        down_kernel, jax.ShapeDtypeStruct((blocks, CAP, quarter), BF16),
        4 * held * width * units, 4 * width * units, 1,
    )(place, hidden, down, down_other)
    back = exchange(out, "expert", by_column)
    own, other = hidden[:, :, :units], hidden[:, :, units:]
    across, mirrored, opposite = cross(other, 1, 0), cross(own, 0, 1), cross(other, 1, 1)
    back, across, mirrored, opposite = lax.optimization_barrier((back, across, mirrored, opposite))

    output, cotan = kernel_call(
        functools.partial(mix_kernel, window),
        (
            jax.ShapeDtypeStruct((tok_count, width), BF16),
            jax.ShapeDtypeStruct((window * QUADS, CAP, quarter), BF16),
        ),
        8 * window * CAP * tok_count * width, 4 * tok_count * width,
    )(spread, loss_weight, back)
    cotan = exchange(cotan, "expert", by_column).reshape(held, quarter)

    groups = reduce_groups(lax.axis_size("pipe"), count)
    cotan = kernel_call(
        turn_kernel, jax.ShapeDtypeStruct((2 * 2, eighth, held), BF16), 0, 6 * held * quarter
    )(cotan)
    cotan = exchange(cotan, ("pipe", "expert"), groups)
    share = kernel_call(
        grads_kernel, jax.ShapeDtypeStruct((QUADS, eighth, units), BF16),
        4 * held * width * units, 4 * width * units, 1,
    )(place, cotan, own, across, mirrored, opposite)
    share = exchange(share, "expert", by_quad).reshape(QUADS * eighth, units).T
    return output[None], share[None]


def solution(mesh):
    in_specs = (
        P("pipe", "expert", None),
        P("pipe", "expert", None),
        P("pipe", "expert", None),
        P("pipe", "expert"),
        P("pipe", None, "expert"),
        P("pipe", None, "expert"),
        P("pipe", "expert", None),
    )
    out_specs = (P("pipe", "expert", None), P("pipe", "expert", None))
    return jax.shard_map(
        per_device, mesh=mesh, in_specs=in_specs, out_specs=out_specs, check_vma=False
    )
```

```python
import functools

import jax
import jax.numpy as jnp
from jax import lax
from jax.experimental import pallas as pl
from jax.experimental.pallas import tpu as pltpu
from jax.sharding import PartitionSpec as P

SPLIT = 8
CAP = 16
QUADS = 4
BF16 = jnp.bfloat16
F32 = jnp.float32
VMEM_LIMIT = 20 * 1024 * 1024


def columns(count):
    return [[i for i in range(count) if i % 2 == side] for side in range(2)]


def quads(count):
    return [
        [base + 2 * place + side for place in range(QUADS)]
        for base in range(0, count, SPLIT)
        for side in range(2)
    ]


def exchange(blocks, axis, groups):
    return lax.all_to_all(blocks, axis, 0, 0, axis_index_groups=groups, tiled=True)


def pass_on(block, step, turn):
    count = lax.axis_size("expert")
    route = []
    for i in range(count):
        place = i % SPLIT // 2
        came = place - step * (turn - 1)
        if 0 <= came < QUADS and 0 <= place + step < QUADS:
            route.append((i, i + 2 * step))
    return lax.ppermute(block, "expert", route)


def neighbour(block):
    count = lax.axis_size("expert")
    return lax.ppermute(block, "expert", [(i, i ^ 1) for i in range(count)])


def swap(block, distance):
    count = lax.axis_size("expert")
    return lax.ppermute(block, "expert", [(i, i ^ 2 * distance) for i in range(count)])


def cross(block, flip_side, flip_pipe):
    pipes, count = lax.axis_size("pipe"), lax.axis_size("expert")
    route = []
    for p in range(pipes):
        for i in range(count):
            other = (p + pipes // 2) % pipes if flip_pipe else p
            route.append((p * count + i, other * count + (i ^ 1 if flip_side else i)))
    return lax.ppermute(block, ("pipe", "expert"), route)


def reduce_groups(pipes, count):
    half = pipes // 2
    return [
        [(p + half * h) * count + i + side for h in range(2) for side in range(2)]
        for p in range(half)
        for i in range(0, count, 2)
    ]


def dot(a, b, dims=((1,), (0,))):
    return lax.dot_general(a, b, (dims, ((), ())), preferred_element_type=F32)


def kernel_call(body, out_shape, flops, moved, scalars=0, left=0, vmem=VMEM_LIMIT, **kwargs):
    def call(*operands):
        specs = [pl.BlockSpec(memory_space=pltpu.SMEM)] * scalars
        specs += [pl.BlockSpec(memory_space=pltpu.VMEM)] * (len(operands) - scalars - left)
        specs += [pl.BlockSpec(memory_space=pl.ANY)] * left
        return pl.pallas_call(
            body,
            out_shape=out_shape,
            in_specs=specs,
            out_specs=jax.tree.map(lambda _: pl.BlockSpec(memory_space=pltpu.VMEM), out_shape),
            compiler_params=pltpu.CompilerParams(vmem_limit_bytes=vmem),
            cost_estimate=pl.CostEstimate(flops=flops, bytes_accessed=moved, transcendentals=0),
            **kwargs,
        )(*operands)

    return call


def quad_of(place_ref):
    return (place_ref[0] & (SPLIT - 1)) >> 1


def relay_kernel(place_ref, w_ref, gate_ref, up_ref, *rest):
    *outs, pair_ref, turned, sems = rest
    copies = [
        pltpu.make_async_copy(a, pair_ref.at[n], sems.at[n]) for n, a in enumerate((gate_ref, up_ref))
    ]
    for copy in copies:
        copy.start()
    quad = quad_of(place_ref)
    turned[...] = w_ref[...].T
    eighth = outs[0].shape[0] // 2
    for d, out in enumerate(outs):
        for h in range(2):
            start = pl.multiple_of((h * QUADS + (quad ^ d)) * eighth, 16)
            out[h * eighth : (h + 1) * eighth, :] = turned[pl.ds(start, eighth), :]
    for copy in copies:
        copy.wait()


def gather_kernel(window, ids, gates, tokens, picked_ref, spread_ref, ids_ref, gates_ref, tok_ref, sems):
    pairs = ((ids, ids_ref), (gates, gates_ref), (tokens, tok_ref))
    copies = [pltpu.make_async_copy(a, b, sems.at[n]) for n, (a, b) in enumerate(pairs)]
    for copy in copies:
        copy.start()
    for copy in copies:
        copy.wait()
    slots, toks = window * CAP, tok_ref.shape[0]
    slot = lax.broadcasted_iota(jnp.int32, (slots, toks), 0)
    expert, nth = slot // CAP, slot % CAP
    weight = jnp.zeros((slots, toks), F32)
    member = jnp.zeros((slots, toks), F32)
    for j in range(ids_ref.shape[0]):
        hit = ids_ref[j : j + 1, :] == expert
        weight = weight + jnp.where(hit, gates_ref[j : j + 1, :], 0.0)
        member = jnp.where(hit, 1.0, member)
    before = lax.broadcasted_iota(jnp.int32, (toks, toks), 0)
    after = lax.broadcasted_iota(jnp.int32, (toks, toks), 1)
    upto = jnp.where(before <= after, 1.0, 0.0).astype(BF16)
    ranking = dot(member.astype(BF16), upto)
    matched = (member > 0.5) & (ranking == (nth + 1).astype(F32))
    spread_ref[...] = jnp.where(matched, weight, 0.0)
    selector = jnp.where(matched, 1.0, 0.0).astype(BF16)
    quarter = picked_ref.shape[2]
    for q in range(QUADS):
        rows = dot(selector, tok_ref[:, q * quarter : (q + 1) * quarter]).astype(BF16)
        for k in range(window):
            picked_ref[k * QUADS + q] = rows[k * CAP : (k + 1) * CAP]


def acts_kernel(place_ref, here, up1, up2, down1, down2, wg, wu, others, acts_ref):
    quad = quad_of(place_ref)
    quarter, units = here.shape[1], wg.shape[1]
    parts = ((here, None, 0), (up1, None, 1), (down1, None, 3), (up2, down2, 2))
    totals = [None] * 4
    for first, second, distance in parts:
        start = pl.multiple_of(((quad + distance) & (QUADS - 1)) * quarter, quarter)
        rows = first[...] if second is None else first[...] + second[...]
        for n, weight in enumerate((wg, wu, others.at[0], others.at[1])):
            part = dot(rows, weight[pl.ds(start, quarter), :])
            totals[n] = part if totals[n] is None else totals[n] + part
    for n in range(4):
        acts_ref[:, n * units : (n + 1) * units] = totals[n]


def hidden_kernel(place_ref, acts, up3, down3, wg, wu, others, hidden_ref):
    quad = quad_of(place_ref)
    quarter, units = up3.shape[1], wg.shape[1]
    last = jnp.where(quad * 2 < QUADS, QUADS - 1, 0)
    start = pl.multiple_of(last * quarter, quarter)
    rows = up3[...] + down3[...]
    both = []
    for n, weight in enumerate((wg, wu, others.at[0], others.at[1])):
        both.append(acts[:, n * units : (n + 1) * units] + dot(rows, weight[pl.ds(start, quarter), :]))
    for side in range(2):
        gate, up = both[2 * side], both[2 * side + 1]
        value = (gate / (1.0 + jnp.exp(-gate)) * up).astype(BF16)
        for s in range(QUADS):
            hidden_ref[s, :, side * units : (side + 1) * units] = value


def down_kernel(place_ref, hidden, down, down_other, out_ref):
    quad = quad_of(place_ref)
    total = None
    for d in range(QUADS):
        slab = jnp.concatenate([down[d], down_other[d]], axis=1)
        part = dot(hidden[quad ^ d], slab, ((1,), (1,)))
        total = part if total is None else total + part
    blocks, cap, quarter = out_ref.shape
    out_ref[...] = total.astype(BF16).reshape(blocks, cap, quarter)


def mix_kernel(window, spread_ref, loss_ref, back, mixed_ref, cotan_ref):
    spread = spread_ref[...]
    high = spread.astype(BF16)
    rest = spread - high.astype(F32)
    middle = rest.astype(BF16)
    low = (rest - middle.astype(F32)).astype(BF16)
    weights = jnp.concatenate([high, middle, low], axis=0)
    chosen = jnp.where(spread > 0.0, 1.0, 0.0).astype(BF16)
    scale = jnp.sum(spread * loss_ref[...], axis=1, keepdims=True)
    eighth = back.shape[2] // 2
    halves = [[], []]
    for q in range(QUADS):
        rows = jnp.concatenate([back[k * QUADS + q] for k in range(window)], axis=0)
        rows = jnp.concatenate([rows, rows, rows], axis=0)
        mixed = dot(weights, rows, ((0,), (0,))).astype(BF16)
        cotan = (scale * dot(chosen, mixed)).astype(BF16)
        for k in range(window):
            cotan_ref[k * QUADS + q] = cotan[k * CAP : (k + 1) * CAP]
        for h in range(2):
            halves[h].append(mixed[:, h * eighth : (h + 1) * eighth])
    mixed_ref[...] = jnp.concatenate(halves[0] + halves[1], axis=1)


def turn_kernel(cotan, out_ref):
    turned = cotan[...].T
    eighth = out_ref.shape[1]
    for h in range(2):
        for side in range(2):
            out_ref[2 * h + side] = turned[h * eighth : (h + 1) * eighth, :]


def grads_kernel(place_ref, cotans, own, across, mirrored, opposite, grads_ref):
    mine = 2 * (place_ref[0] // SPLIT) + (place_ref[0] & 1)
    units = own.shape[2]
    total = None
    for flip, hidden in enumerate((own, across, mirrored, opposite)):
        slab = jnp.concatenate([hidden[s] for s in range(QUADS)], axis=1)
        part = dot(cotans[mine ^ flip], slab)
        total = part if total is None else total + part
    for s in range(QUADS):
        grads_ref[s] = total[:, s * units : (s + 1) * units].astype(BF16)


def per_device(tokens, expert_ids, gates, loss_weight, w_gate, w_up, w_down):
    tok_count, width = tokens.shape[1:]
    choices = gates.shape[2]
    units = w_down.shape[1]
    count = lax.axis_size("expert")
    window = count // SPLIT
    quarter, eighth = width // QUADS, width // (2 * QUADS)
    place = lax.axis_index("expert")
    mirror = lax.axis_index("pipe") // (lax.axis_size("pipe") // 2)
    place = (place % SPLIT + SPLIT * mirror).reshape(1)
    by_column, by_quad = columns(count), quads(count)
    blocks = count // 2
    held = blocks * CAP

    *down, gate_up = kernel_call(
        relay_kernel,
        (jax.ShapeDtypeStruct((quarter, units), BF16),) * QUADS
        + (jax.ShapeDtypeStruct((2, width, units), BF16),),
        0, 12 * width * units, 1, left=2, vmem=3 * VMEM_LIMIT,
        scratch_shapes=[pltpu.VMEM((width, units), BF16), pltpu.SemaphoreType.DMA((2,))],
    )(place, w_down[0], w_gate[0], w_up[0])
    others = neighbour(gate_up)
    down = [down[0]] + [swap(down[d], d) for d in range(1, QUADS)]

    picked, spread = kernel_call(
        functools.partial(gather_kernel, window),
        (
            jax.ShapeDtypeStruct((window * QUADS, CAP, quarter), BF16),
            jax.ShapeDtypeStruct((window * CAP, tok_count), F32),
        ),
        2 * window * CAP * tok_count * width, 3 * tok_count * width, left=3,
        scratch_shapes=[
            pltpu.VMEM((choices, tok_count), jnp.int32),
            pltpu.VMEM((choices, tok_count), F32),
            pltpu.VMEM((tok_count, width), BF16),
            pltpu.SemaphoreType.DMA((3,)),
        ],
    )(expert_ids[0].T, gates[0].T, tokens[0])
    once = lax.optimization_barrier(jnp.int32(1))
    rows = lax.cond(once > 0, lambda b: exchange(b, "expert", by_column), lambda b: b, picked)
    rows = rows.reshape(held, quarter)
    rows, others, *down = lax.optimization_barrier((rows, others, *down))
    down = jnp.stack(down)
    down_other = neighbour(down)
    ups, downs = [rows], [rows]
    for turn in range(1, QUADS):
        ups.append(pass_on(ups[-1], 1, turn))
        downs.append(pass_on(downs[-1], -1, turn))
    weights = (w_gate[0], w_up[0], others)
    acts = kernel_call(
        acts_kernel, jax.ShapeDtypeStruct((held, 4 * units), F32),
        8 * held * width * units, 8 * width * units, 1,
    )(place, rows, downs[1], downs[2], ups[1], ups[2], *weights)
    hidden = kernel_call(
        hidden_kernel, jax.ShapeDtypeStruct((QUADS, held, 2 * units), BF16),
        2 * held * width * units, 2 * width * units, 1,
    )(place, acts, downs[3], ups[3], *weights)
    hidden, down_other = lax.optimization_barrier((hidden, down_other))
    hidden = exchange(hidden, "expert", by_quad)
    out = kernel_call(
        down_kernel, jax.ShapeDtypeStruct((blocks, CAP, quarter), BF16),
        4 * held * width * units, 4 * width * units, 1,
    )(place, hidden, down, down_other)
    back = exchange(out, "expert", by_column)
    own, other = hidden[:, :, :units], hidden[:, :, units:]
    across, mirrored, opposite = cross(other, 1, 0), cross(own, 0, 1), cross(other, 1, 1)
    back, across, mirrored, opposite = lax.optimization_barrier((back, across, mirrored, opposite))

    output, cotan = kernel_call(
        functools.partial(mix_kernel, window),
        (
            jax.ShapeDtypeStruct((tok_count, width), BF16),
            jax.ShapeDtypeStruct((window * QUADS, CAP, quarter), BF16),
        ),
        8 * window * CAP * tok_count * width, 4 * tok_count * width,
    )(spread, loss_weight, back)
    cotan = exchange(cotan, "expert", by_column).reshape(held, quarter)

    groups = reduce_groups(lax.axis_size("pipe"), count)
    cotan = kernel_call(
        turn_kernel, jax.ShapeDtypeStruct((2 * 2, eighth, held), BF16), 0, 6 * held * quarter
    )(cotan)
    cotan = exchange(cotan, ("pipe", "expert"), groups)
    share = kernel_call(
        grads_kernel, jax.ShapeDtypeStruct((QUADS, eighth, units), BF16),
        4 * held * width * units, 4 * width * units, 1,
    )(place, cotan, own, across, mirrored, opposite)
    share = exchange(share, "expert", by_quad).reshape(QUADS * eighth, units).T
    return output[None], share[None]


def solution(mesh):
    in_specs = (
        P("pipe", "expert", None),
        P("pipe", "expert", None),
        P("pipe", "expert", None),
        P("pipe", "expert"),
        P("pipe", None, "expert"),
        P("pipe", None, "expert"),
        P("pipe", "expert", None),
    )
    out_specs = (P("pipe", "expert", None), P("pipe", "expert", None))
    return jax.shard_map(
        per_device, mesh=mesh, in_specs=in_specs, out_specs=out_specs, check_vma=False
    )
```
